32 devices in a mesh: parts: 2 (over y), col: 4 (over z), row: 4 (over x, core).
Axes of the slice: x: 2, y: 2, z: 4, core: 2. Of those that a mesh axis runs over, the one named last changes fastest.
Arguments:
- x_tiles: bfloat16 [8, 4, 8, 128, 128], P(('parts', 'row'), 'col'), parts along dimension 0, may hold values from -1.796875 to 1.796875
- x_index: int32 [8, 4, 2, 8], P(('parts', 'row'), 'col'), parts along dimension 0, may hold values from -1 to 3, as said below
- square_index: int32 [8, 4, 2, 8], P(('parts', 'row'), 'col'), parts along dimension 0, may hold values from -1 to 3, as said below
- new_index: int32 [8, 4, 2, 8], P(('parts', 'row'), 'col'), parts along dimension 0, may hold values from -1 to 3, as said below
Outputs:
- squared: bfloat16 [8, 4, 8, 128, 128], P(('parts', 'row'), 'col'), parts along dimension 0
- refined: bfloat16 [8, 4, 8, 128, 128], P(('parts', 'row'), 'col'), parts along dimension 0
The draws below stay inside these ranges and needn't reach their ends.
There are 2 independent parts, one for each index of `parts`. The reference program is written for one: setup_inputs(seed, part) draws one part's arguments, and reference() takes and returns one part's arrays. A program takes and returns all parts, laid end to end along the dimension named above; each array names one. Nothing has to cross between parts.
Inputs may be any that keep to these rules, and one draw needn't show every extreme that they name: `x_index`: entry [r, c, 0, s] is the tile row (0 to 3) and [r, c, 1, s] the tile column (0 to 3) of slot s inside block (r, c); both are -1 for an empty slot, and the filled slots of a block come first and name distinct tiles. No tile row has more than 2 tiles in one block, and some row has exactly 2; some block fills all 8 slots. `square_index`: same layout as x_index. Every named tile (i, j) has some k with tiles (i, k) and (k, j) in X's pattern; no tile row has more than 2 tiles in one block; filled slots name distinct tiles, empty ones are -1 in both entries. `new_index`: same layout as x_index. Every named tile (i, j) has some k with tile (i, k) in X's pattern and (k, j) in square_index; no tile row has more than 2 tiles in one block; filled slots name distinct tiles, empty ones are -1 in both entries.
All inputs are finite; a program needn't handle non-finite values.
Results may differ from the reference program's by a relative error of at most 0.0051.
Values may be sent and summed in bfloat16 or wider, within the bound.
A program may use at most 64 MiB of HBM per device.

```python
import jax
import jax.numpy as jnp
from jax import lax

TILE = 128
ROW_MOST = 2
BLOCK_COLS = 4
SLOTS = 8
TILES = 16
BLOCK_ROWS = 4
N_COL = 4
N_ROW = 4


def spread(local_rows, local_cols):
    col_blocks = TILES // BLOCK_COLS
    block_ids = jnp.arange(local_rows.shape[0], dtype=jnp.int32)
    global_rows = (block_ids // col_blocks)[:, None] * BLOCK_ROWS + jnp.maximum(local_rows, 0)
    global_cols = (block_ids % col_blocks)[:, None] * BLOCK_COLS + jnp.maximum(local_cols, 0)
    weights = (local_rows >= 0).astype(jnp.int32)
    empty_mask = jnp.zeros((TILES, TILES), jnp.int32)
    return empty_mask.at[global_rows.reshape(-1), global_cols.reshape(-1)].add(weights.reshape(-1))


def sift(key, counted, salt):
    row_blocks = TILES // BLOCK_ROWS
    col_blocks = TILES // BLOCK_COLS
    block_total = row_blocks * col_blocks
    scores = (jax.random.permutation(jax.random.fold_in(key, salt), TILES * TILES).astype(jnp.int32) + 1).reshape(TILES, TILES)
    scores = scores * (counted > 0).astype(jnp.int32)
    blocked = scores.reshape(row_blocks, BLOCK_ROWS, col_blocks, BLOCK_COLS).transpose(0, 2, 1, 3)
    blocked = blocked.reshape(block_total, BLOCK_ROWS, BLOCK_COLS)
    row_best, row_where = lax.top_k(blocked, ROW_MOST)
    best_flat = row_best.reshape(block_total, BLOCK_ROWS * ROW_MOST)
    where_flat = row_where.reshape(block_total, BLOCK_ROWS * ROW_MOST).astype(jnp.int32)
    top_scores, top_places = lax.top_k(best_flat, SLOTS)
    live_slot = top_scores > 0
    out_rows = jnp.where(live_slot, top_places // ROW_MOST, -1).astype(jnp.int32)
    out_cols = jnp.where(live_slot, jnp.take_along_axis(where_flat, top_places, axis=1), -1).astype(jnp.int32)
    return (out_rows, out_cols)


def layout(key):
    row_blocks = TILES // BLOCK_ROWS
    col_blocks = TILES // BLOCK_COLS
    block_total = row_blocks * col_blocks
    row_count = SLOTS // ROW_MOST
    block_keys = jax.random.split(jax.random.fold_in(key, 101), block_total)

    def one_block(block_key):
        row_key, col_key = jax.random.split(block_key)
        chosen_rows = jax.random.permutation(row_key, BLOCK_ROWS)[:row_count]
        col_keys = jax.random.split(col_key, row_count)
        chosen_cols = jax.vmap(lambda inner_key: jax.random.permutation(inner_key, BLOCK_COLS)[:ROW_MOST])(col_keys)
        return (chosen_rows, chosen_cols)
    block_rows, block_cols = jax.vmap(one_block)(block_keys)
    least_used = max(row_count, SLOTS * 3 // 4)
    used_slots = jax.random.randint(jax.random.fold_in(key, 102), (block_total,), least_used, SLOTS + 1)
    fullest = jax.random.randint(jax.random.fold_in(key, 103), (), 0, block_total)
    block_ids = jnp.arange(block_total, dtype=jnp.int32)
    used_slots = jnp.where(block_ids == fullest, SLOTS, used_slots)
    slot_ids = jnp.arange(SLOTS, dtype=jnp.int32)
    live_slot = slot_ids[None, :] < used_slots[:, None]
    slot_rows = block_rows[:, slot_ids // ROW_MOST]
    slot_cols = block_cols[:, slot_ids // ROW_MOST, slot_ids % ROW_MOST]
    x_rows = jnp.where(live_slot, slot_rows, -1).astype(jnp.int32)
    x_cols = jnp.where(live_slot, slot_cols, -1).astype(jnp.int32)
    x_mask = spread(x_rows, x_cols)
    square_rows, square_cols = sift(key, jnp.dot(x_mask, x_mask), 104)
    square_mask = spread(square_rows, square_cols)
    new_rows, new_cols = sift(key, jnp.dot(x_mask, square_mask), 105)

    def packed(pair_rows, pair_cols):
        return jnp.stack([pair_rows, pair_cols], axis=1).reshape(row_blocks, col_blocks, 2, SLOTS)
    return (packed(x_rows, x_cols), packed(square_rows, square_cols), packed(new_rows, new_cols))


def draw_x_index(key, part):
    shared = layout(key)
    return shared[0]


def draw_square_index(key, part):
    shared = layout(key)
    return shared[1]


def draw_new_index(key, part):
    shared = layout(key)
    return shared[2]


def block_levels(rng, dims, cuts, smallest, top_value):
    def one(dim, parts):
        steps = jax.random.uniform(jax.random.fold_in(jax.random.fold_in(rng, 6), dim), (parts,), jnp.float32, smallest / len(cuts), top_value / len(cuts))
        return jnp.repeat(jnp.exp(steps), dims[dim] // parts).reshape((-1,) + (1,) * (len(dims) - dim - 1))

    gain = one(*cuts[0])
    for cut in cuts[1:]:
        gain = gain * one(*cut)
    return gain


def scatter_about(own_key, extent, width, limit, pieces=(), held_as=jnp.bfloat16):
    result = width * jax.random.normal(own_key, extent, jnp.float32)
    if pieces:
        result = result * block_levels(own_key, extent, pieces, -0.22, 0.18)
    return jnp.clip(result, -limit, limit).astype(held_as)


def setup_inputs(seed: int = 0, part: int = 0) -> dict:
    splits = jax.random.split(jax.random.key(seed), 5)
    own_keys = jax.random.split(jax.random.fold_in(splits[4], part), 5)
    x_tiles = scatter_about(own_keys[0], (N_ROW, N_COL, SLOTS, TILE, TILE), 0.3, 1.796875, ((0, 4), (1, 4)))
    x_index = draw_x_index(jax.random.fold_in(jax.random.fold_in(splits[4], part), 71), part)
    square_index = draw_square_index(jax.random.fold_in(jax.random.fold_in(splits[4], part), 71), part)
    new_index = draw_new_index(jax.random.fold_in(jax.random.fold_in(splits[4], part), 71), part)
    return {"x_tiles": x_tiles, "x_index": x_index, "square_index": square_index, "new_index": new_index}


def block_step(running, a_tiles, a_index, k_block, b_tiles, b_row, b_col, target):
    slot_count = a_tiles.shape[0]
    panel_count = b_row.shape[0]
    a_row = a_index[0]
    a_col = a_index[1]
    a_live = a_row >= 0
    slot_ids = jnp.arange(slot_count, dtype=jnp.int32)
    same_row = (a_row[:, None] == a_row[None, :]) & a_live[None, :] & (slot_ids[None, :] < slot_ids[:, None])
    a_rank = jnp.sum(same_row.astype(jnp.int32), axis=1)
    c_row = target[0]
    c_col = target[1]
    rank_ids = jnp.arange(ROW_MOST, dtype=jnp.int32)
    chosen = (a_row[None, None, :] == c_row[:, None, None]) & a_live[None, None, :]
    chosen = chosen & (a_rank[None, None, :] == rank_ids[None, :, None]) & (c_row[:, None, None] >= 0)
    chosen_int = chosen.astype(jnp.int32)
    a_found = jnp.sum(chosen_int, axis=2) > 0
    a_pick = jnp.sum(chosen_int * slot_ids[None, None, :], axis=2) + jnp.where(a_found, 0, slot_count).astype(jnp.int32)
    k_row = k_block * BLOCK_COLS + jnp.sum(chosen_int * a_col[None, None, :], axis=2)
    panel_ids = jnp.arange(panel_count, dtype=jnp.int32)
    matched = (b_row[None, None, :] == k_row[:, :, None]) & (b_col[None, None, :] == c_col[:, None, None]) & a_found[:, :, None]
    matched_int = matched.astype(jnp.int32)
    b_found = jnp.sum(matched_int, axis=2) > 0
    b_pick = jnp.sum(matched_int * panel_ids[None, None, :], axis=2) + jnp.where(b_found, 0, panel_count).astype(jnp.int32)
    padded = jnp.concatenate([a_tiles, jnp.zeros((1,) + a_tiles.shape[1:], a_tiles.dtype)], axis=0)
    left_tiles = padded[a_pick].astype(jnp.float32)
    right_tiles = b_tiles[b_pick].astype(jnp.float32)
    return running + jnp.einsum("cmij,cmjk->cik", left_tiles, right_tiles, precision=lax.Precision.HIGHEST)


def prepare_panel(panel_tiles, panel_index, row_tiles):
    block_ids = jnp.arange(panel_tiles.shape[0], dtype=jnp.int32)
    raw_rows = panel_index[:, 0, :]
    b_row = jnp.where(raw_rows >= 0, block_ids[:, None] * row_tiles + raw_rows, -1).reshape(-1)
    b_col = panel_index[:, 1, :].reshape(-1)
    flat_tiles = panel_tiles.reshape((-1,) + panel_tiles.shape[2:])
    padded = jnp.concatenate([flat_tiles, jnp.zeros((1,) + flat_tiles.shape[1:], flat_tiles.dtype)], axis=0)
    return padded, b_row, b_col


def product(a_tiles, a_index, b_tiles, b_index, c_index):
    def one_block(block_id):
        row_id = block_id // N_COL
        col_id = block_id % N_COL
        panel_tiles = lax.dynamic_index_in_dim(b_tiles, col_id, 1, keepdims=False)
        panel_index = lax.dynamic_index_in_dim(b_index, col_id, 1, keepdims=False)
        padded, b_row, b_col = prepare_panel(panel_tiles, panel_index, BLOCK_ROWS)
        left_rows = lax.dynamic_index_in_dim(a_tiles, row_id, 0, keepdims=False)
        left_index = lax.dynamic_index_in_dim(a_index, row_id, 0, keepdims=False)
        target = lax.dynamic_index_in_dim(lax.dynamic_index_in_dim(c_index, row_id, 0, keepdims=False), col_id, 0, keepdims=False)

        def absorb(k_block, running):
            k_block = k_block.astype(jnp.int32)
            return block_step(running, left_rows[k_block], left_index[k_block], k_block, padded, b_row, b_col, target)

        start = jnp.zeros(a_tiles.shape[2:], jnp.float32)
        return lax.fori_loop(0, N_COL, absorb, start)

    sums = lax.map(one_block, jnp.arange(N_ROW * N_COL, dtype=jnp.int32))
    return sums.reshape(a_tiles.shape[:2] + sums.shape[1:])


def pick_own(own_tiles, own_index, target):
    slot_count = own_tiles.shape[0]
    slot_ids = jnp.arange(slot_count, dtype=jnp.int32)
    matched = (own_index[0][None, :] == target[0][:, None]) & (own_index[1][None, :] == target[1][:, None]) & (own_index[0][None, :] >= 0)
    matched_int = matched.astype(jnp.int32)
    found = jnp.sum(matched_int, axis=1) > 0
    picked = jnp.sum(matched_int * slot_ids[None, :], axis=1) + jnp.where(found, 0, slot_count).astype(jnp.int32)
    padded = jnp.concatenate([own_tiles, jnp.zeros((1,) + own_tiles.shape[1:], own_tiles.dtype)], axis=0)
    return padded[picked]


def reference(x_tiles, x_index, square_index, new_index):
    square_sum = product(x_tiles, x_index, x_tiles, x_index, square_index)
    squared = square_sum.astype(jnp.bfloat16)
    refined_sum = product(x_tiles, x_index, squared, square_index, new_index)
    own_part = jax.vmap(jax.vmap(pick_own))(x_tiles, x_index, new_index)
    refined = (1.5 * own_part.astype(jnp.float32) - 0.5 * refined_sum).astype(jnp.bfloat16)
    return squared, refined
```

```python
import functools

import jax
import jax.numpy as jnp
from jax import lax
from jax.experimental import pallas as pl
from jax.experimental.pallas import tpu as pltpu
from jax.sharding import PartitionSpec as P

MESH = pl.DeviceIdType.MESH
ROW_MOST = 2
BLOCK_COLS = 4
META = 16
FEW = 8
BF16 = jnp.bfloat16
F32 = jnp.float32


def loop(count, body):
    if count <= FEW:
        for i in range(count):
            body(i)
    else:
        lax.fori_loop(0, count, lambda i, _: (body(i), 0)[1], 0)


class Plan:
    def __init__(self, n_col, n_row, slots, tile, chunks):
        self.n_col, self.n_row, self.slots, self.tile = n_col, n_row, slots, tile
        self.rows = BLOCK_COLS * n_col // n_row
        self.canonical = self.rows * ROW_MOST <= slots
        self.chunks = chunks if self.canonical and self.rows % chunks == 0 else 1
        self.pos = self.rows * ROW_MOST if self.canonical else slots
        self.rc = self.rows // self.chunks
        self.pc = self.pos // self.chunks
        self.ch = self.pc * tile + META
        self.places = self.rows * BLOCK_COLS
        self.small = self.rows <= FEW and n_col <= FEW
        self.width = BLOCK_COLS * tile
        assert self.pc <= META and self.places <= 256 and n_row % 2 == 0


def slot_keys(plan, idx):
    rows = [idx[0, 0, 0, s] for s in range(plan.slots)]
    out = []
    if not plan.canonical:
        for s in range(plan.slots):
            out.append((s, jnp.where(rows[s] >= 0, rows[s] * BLOCK_COLS + idx[0, 0, 1, s], -1)))
        return out
    for i in range(plan.rows):
        found = [jnp.int32(plan.slots)] * ROW_MOST
        for s in reversed(range(plan.slots)):
            hit = rows[s] == i
            found = [
                jnp.where(hit, found[k - 1] if k else jnp.int32(s), found[k]) for k in range(ROW_MOST)
            ]
        for slot in found:
            live = slot < plan.slots
            slot = jnp.minimum(slot, plan.slots - 1)
            out.append((slot, jnp.where(live, i * BLOCK_COLS + idx[0, 0, 1, slot], -1)))
    return out


def out_keys(plan, idx):
    rows = [idx[0, 0, 0, s] for s in range(plan.slots)]
    return [
        jnp.where(rows[s] >= 0, rows[s] * BLOCK_COLS + idx[0, 0, 1, s], plan.places)
        for s in range(plan.slots)
    ]


def meta_of(plan, keys):
    place = lax.broadcasted_iota(jnp.int32, (META, plan.tile), 0)
    meta = jnp.full((META, plan.tile), -1, jnp.int32)
    for p, key in enumerate(keys):
        meta = jnp.where(place == p, key, meta)
    return meta.astype(F32).astype(BF16)


def row_tiles(plan, chunk, i, il):
    t = plan.tile
    meta = chunk[plan.pc * t : plan.pc * t + META, :].astype(F32)
    cands = range(il * ROW_MOST, (il + 1) * ROW_MOST) if plan.canonical else range(plan.pc)
    out = []
    for j in range(BLOCK_COLS):
        key = jnp.asarray(i * BLOCK_COLS + j, jnp.int32).astype(F32)
        total = None
        for p in cands:
            here = jnp.broadcast_to(meta[p : p + 1, :], (META, t)) == key
            mask = jnp.where(here, 1.0, 0.0).astype(BF16)
            part = chunk[p * t : (p + 1) * t, :].reshape(t // META, META, t) * mask[None]
            total = part if total is None else total + part
        out.append(total.reshape(t, t))
    return out


def kernel(
    plan,
    x_ref, xi_ref, si_ref, ni_ref,
    sq_ref, rf_ref,
    pk, sk, zbuf, rbuf, sbuf, bd, ld, acc, xt, *rest,
):
    if plan.small:
        sd, acc2, *sems = rest
    else:
        sd, acc2, sems = bd, acc, rest
    zrecv, up_send, dn_send, rrecv, pair_send, cross_send, relay_send, srecv, spair_send, scross_send, srelay_send = sems
    n_col, n_row, t, chunks = plan.n_col, plan.n_row, plan.tile, plan.chunks
    c = lax.axis_index("col")
    r = lax.axis_index("row")
    pair = r + 1 - 2 * lax.rem(r, 2)
    hops = range(1, n_row // 2)
    crosses = [lax.rem(r + 2 * m, n_row) for m in hops]
    sources = [lax.rem(r + n_row - 2 * m, n_row) for m in hops]
    relayed = [lax.rem(pair + n_row - 2 * m, n_row) for m in hops]

    barrier = pltpu.get_barrier_semaphore()

    @pl.when(c > 0)
    def _():
        pl.semaphore_signal(barrier, inc=1, device_id={"col": c - 1}, device_id_type=MESH)

    @pl.when(c < n_col - 1)
    def _():
        pl.semaphore_signal(barrier, inc=1, device_id={"col": c + 1}, device_id_type=MESH)

    for other in [pair] + crosses:
        pl.semaphore_signal(barrier, inc=1, device_id={"row": other}, device_id_type=MESH)

    x_keys = slot_keys(plan, xi_ref)
    for g in range(chunks):
        mine = x_keys[g * plan.pc : (g + 1) * plan.pc]
        for p, (slot, _) in enumerate(mine):
            pk[g, p * t : (p + 1) * t, :] = x_ref[0, 0, slot]
        pk[g, plan.pc * t : plan.ch, :] = meta_of(plan, [key for _, key in mine])

    inner = jnp.where(c > 0, 1, 0) + jnp.where(c < n_col - 1, 1, 0)
    pl.semaphore_wait(barrier, inner + 1 + len(crosses))

    def col_copy(src, kb, g, send, to):
        return pltpu.make_async_remote_copy(
            src_ref=src, dst_ref=zbuf.at[kb, g], send_sem=send.at[kb, g], recv_sem=zrecv.at[kb, g],
            device_id={"col": to}, device_id_type=MESH,
        )

    def row_copy(src, dst, origin, g, send, recv, to):
        return pltpu.make_async_remote_copy(
            src_ref=src, dst_ref=dst.at[origin, g], send_sem=send, recv_sem=recv.at[origin, g],
            device_id={"row": to}, device_id_type=MESH,
        )

    def send_row(src, dst, g, pair_sem, cross_sem, recv):
        for m, to in enumerate(crosses):
            row_copy(src.at[g], dst, r, g, cross_sem.at[m, g], recv, to).start()
        row_copy(src.at[g], dst, r, g, pair_sem.at[g], recv, pair).start()

    def take_cross(dst, g, relay_sem, recv):
        for m, origin in enumerate(sources):
            hop = row_copy(dst.at[origin, g], dst, origin, g, relay_sem.at[m, g], recv, pair)
            hop.wait_recv()
            hop.start()

    def take_pair(dst, g, recv, relay_sem):
        row_copy(dst.at[pair, g], dst, pair, g, relay_sem.at[0, g], recv, pair).wait_recv()

    def take_relayed(dst, g, recv, relay_sem):
        for origin in relayed:
            row_copy(dst.at[origin, g], dst, origin, g, relay_sem.at[0, g], recv, pair).wait_recv()

    def end_row(src, dst, g, pair_sem, cross_sem, relay_sem, recv):
        row_copy(src.at[g], dst, r, g, pair_sem.at[g], recv, pair).wait_send()
        for m, to in enumerate(crosses):
            row_copy(src.at[g], dst, r, g, cross_sem.at[m, g], recv, to).wait_send()
        for m, origin in enumerate(sources):
            row_copy(dst.at[origin, g], dst, origin, g, relay_sem.at[m, g], recv, pair).wait_send()

    for g in range(chunks):
        @pl.when(c < n_col - 1)
        def _():
            col_copy(pk.at[g], c, g, up_send, c + 1).start()

        @pl.when(c > 0)
        def _():
            col_copy(pk.at[g], c, g, dn_send, c - 1).start()

        send_row(pk, rbuf, g, pair_send, cross_send, rrecv)

    acc[plan.places] = jnp.zeros((t, t), F32)
    acc2[plan.places] = jnp.zeros((t, t), F32)
    xt[plan.places] = jnp.zeros((t, t), BF16)

    def forward(d, g):
        @pl.when(c >= d)
        def _():
            col_copy(zbuf.at[c - d, g], c - d, g, up_send, c).wait_recv()

            @pl.when(c < n_col - 1)
            def _():
                col_copy(zbuf.at[c - d, g], c - d, g, up_send, c + 1).start()

        @pl.when(c + d < n_col)
        def _():
            col_copy(zbuf.at[c + d, g], c + d, g, dn_send, c).wait_recv()

            @pl.when(c > 0)
            def _():
                col_copy(zbuf.at[c + d, g], c + d, g, dn_send, c - 1).start()

    def unpack(chunk, origin, g, dense):
        def one(il):
            i = g * plan.rc + il
            for j, tile in enumerate(row_tiles(plan, chunk, i, il)):
                dense[origin * plan.rows + i, :, j * t : (j + 1) * t] = tile
        loop(plan.rc, one)

    def right_of(dense, kb):
        return dense[pl.ds(kb * BLOCK_COLS, BLOCK_COLS)].reshape(plan.width, plan.width)

    def add(into, i, product, first):
        for j in range(BLOCK_COLS):
            part = product[:, j * t : (j + 1) * t]
            if first:
                into[i * BLOCK_COLS + j] = part
            else:
                into[i * BLOCK_COLS + j] += part

    def multiply(chunk, kb, g, dense, into, first):
        def one(il):
            i = g * plan.rc + il
            left = jnp.concatenate(row_tiles(plan, chunk, i, il), axis=1)
            add(into, i, jnp.dot(left, right_of(dense, kb), preferred_element_type=F32), first)

        if not plan.small:
            loop(plan.rc, one)
            return
        for il in range(plan.rc):
            for j, tile in enumerate(row_tiles(plan, chunk, g * plan.rc + il, il)):
                ld[kb, g * plan.rc + il, :, j * t : (j + 1) * t] = tile
        left = ld[kb, g * plan.rc : (g + 1) * plan.rc].reshape(plan.rc * t, plan.width)
        product = jnp.dot(left, right_of(dense, kb), preferred_element_type=F32)
        for il in range(plan.rc):
            add(into, g * plan.rc + il, product[il * t : (il + 1) * t], first)

    def multiply_pair(d, g, dense, into):
        @pl.when(c >= d)
        def _():
            multiply(zbuf.at[c - d, g], c - d, g, dense, into, False)

        @pl.when(c + d < n_col)
        def _():
            multiply(zbuf.at[c + d, g], c + d, g, dense, into, False)

    for g in range(chunks):
        take_cross(rbuf, g, relay_send, rrecv)
        forward(1, g)
    for g in range(chunks):
        unpack(pk.at[g], r, g, bd)
        take_pair(rbuf, g, rrecv, relay_send)
        unpack(rbuf.at[pair, g], pair, g, bd)
        for origin in sources:
            unpack(rbuf.at[origin, g], origin, g, bd)

        def keep(il):
            i = g * plan.rc + il
            for j in range(BLOCK_COLS):
                xt[i * BLOCK_COLS + j] = bd[r * plan.rows + i, :, j * t : (j + 1) * t]
        loop(plan.rc, keep)
    for g in range(chunks):
        take_relayed(rbuf, g, rrecv, relay_send)
        for origin in relayed:
            unpack(rbuf.at[origin, g], origin, g, bd)
    for g in range(chunks):
        multiply(pk.at[g], c, g, bd, acc, True)

    s_keys = slot_keys(plan, si_ref)

    def send_square(g):
        mine = s_keys[g * plan.pc : (g + 1) * plan.pc]
        for p, (_, key) in enumerate(mine):
            sk[g, p * t : (p + 1) * t, :] = acc[jnp.where(key < 0, plan.places, key)].astype(BF16)
        sk[g, plan.pc * t : plan.ch, :] = meta_of(plan, [key for _, key in mine])
        send_row(sk, sbuf, g, spair_send, scross_send, srecv)

    for g in range(chunks):
        multiply_pair(1, g, bd, acc)

    if plan.small:
        for d in range(2, n_col):
            for g in range(chunks):
                forward(d, g)
                multiply_pair(d, g, bd, acc)
                if d == n_col - 1:
                    send_square(g)
        if n_col == 2:
            for g in range(chunks):
                send_square(g)
    else:
        def later(d):
            for g in range(chunks):
                forward(d, g)
                multiply_pair(d, g, bd, acc)
        lax.fori_loop(2, n_col, lambda d, _: (later(d), 0)[1], 0)
        for g in range(chunks):
            send_square(g)

    for s, key in enumerate(out_keys(plan, si_ref)):
        sq_ref[0, 0, s] = acc[key].astype(BF16)

    for g in range(chunks):
        unpack(sk.at[g], r, g, sd)
        take_pair(sbuf, g, srecv, srelay_send)
        unpack(sbuf.at[pair, g], pair, g, sd)
        take_cross(sbuf, g, srelay_send, srecv)
        for origin in sources:
            unpack(sbuf.at[origin, g], origin, g, sd)
    for g in range(chunks):
        take_relayed(sbuf, g, srecv, srelay_send)
        for origin in relayed:
            unpack(sbuf.at[origin, g], origin, g, sd)

    if plan.small:
        for kb in range(n_col):
            left = ld[kb].reshape(plan.rows * t, plan.width)
            product = jnp.dot(left, right_of(sd, kb), preferred_element_type=F32)
            for i in range(plan.rows):
                add(acc2, i, product[i * t : (i + 1) * t], kb == 0)
    else:
        for g in range(chunks):
            multiply(pk.at[g], c, g, sd, acc2, True)

            def again(d):
                multiply_pair(d, g, sd, acc2)
            lax.fori_loop(1, n_col, lambda d, _: (again(d), 0)[1], 0)

    for s, key in enumerate(out_keys(plan, ni_ref)):
        rf_ref[0, 0, s] = (1.5 * xt[key].astype(F32) - 0.5 * acc2[key]).astype(BF16)

    for g in range(chunks):
        end_row(pk, rbuf, g, pair_send, cross_send, relay_send, rrecv)
        end_row(sk, sbuf, g, spair_send, scross_send, srelay_send, srecv)

        @pl.when(c < n_col - 1)
        def _():
            col_copy(pk.at[g], c, g, up_send, c + 1).wait_send()

        @pl.when(c > 0)
        def _():
            col_copy(pk.at[g], c, g, dn_send, c - 1).wait_send()

        def sent(d):
            @pl.when(jnp.logical_and(c >= d, c < n_col - 1))
            def _():
                col_copy(zbuf.at[c - d, g], c - d, g, up_send, c + 1).wait_send()

            @pl.when(jnp.logical_and(c + d < n_col, c > 0))
            def _():
                col_copy(zbuf.at[c + d, g], c + d, g, dn_send, c - 1).wait_send()
        if plan.small:
            for d in range(1, n_col):
                sent(d)
        else:
            lax.fori_loop(1, n_col, lambda d, _: (sent(d), 0)[1], 0)


CHUNKS = 2


def solution(mesh):
    n_col, n_row = mesh.shape["col"], mesh.shape["row"]

    def shards(x_tiles, x_index, square_index, new_index):
        slots, t = x_tiles.shape[2], x_tiles.shape[3]
        plan = Plan(n_col, n_row, slots, t, CHUNKS)
        k, ch, g = plan.rows * n_row, plan.ch, plan.chunks
        half = max(n_row // 2 - 1, 1)
        scratch = [
            pltpu.VMEM((g, ch, t), BF16),
            pltpu.VMEM((g, ch, t), BF16),
            pltpu.VMEM((n_col, g, ch, t), BF16),
            pltpu.VMEM((n_row, g, ch, t), BF16),
            pltpu.VMEM((n_row, g, ch, t), BF16),
            pltpu.VMEM((k, t, plan.width), BF16),
            pltpu.VMEM((n_col, plan.rows, t, plan.width) if plan.small else (1, 1, 16, t), BF16),
            pltpu.VMEM((plan.places + 1, t, t), F32),
            pltpu.VMEM((plan.places + 1, t, t), BF16),
        ]
        if plan.small:
            scratch += [
                pltpu.VMEM((k, t, plan.width), BF16),
                pltpu.VMEM((plan.places + 1, t, t), F32),
            ]
        dma = pltpu.SemaphoreType.DMA
        scratch += [dma((n_col, g))] * 3
        scratch += [dma((n_row, g)), dma((g,)), dma((half, g)), dma((half, g))] * 2
        shape = jax.ShapeDtypeStruct(x_tiles.shape, BF16)
        vmem = pl.BlockSpec(memory_space=pltpu.VMEM)
        smem = pl.BlockSpec(memory_space=pltpu.SMEM)
        return pl.pallas_call(
            functools.partial(kernel, plan),
            out_shape=(shape, shape),
            in_specs=[vmem, smem, smem, smem],
            out_specs=(vmem, vmem),
            scratch_shapes=scratch,
            compiler_params=pltpu.CompilerParams(
                collective_id=0, has_side_effects=True,
                vmem_limit_bytes=(24 if plan.small else 56) * 2**20,
            ),
        )(x_tiles, x_index, square_index, new_index)

    tiles = P(("parts", "row"), "col", None, None, None)
    index = P(("parts", "row"), "col", None, None)
    return jax.shard_map(
        shards, mesh=mesh, in_specs=(tiles, index, index, index), out_specs=(tiles, tiles), check_vma=False,
    )
```

```python
import functools

import jax
import jax.numpy as jnp
from jax import lax
from jax.experimental import pallas as pl
from jax.experimental.pallas import tpu as pltpu
from jax.sharding import PartitionSpec as P

MESH = pl.DeviceIdType.MESH
ROW_MOST = 2
BLOCK_COLS = 4
META = 16
FEW = 8
BF16 = jnp.bfloat16
F32 = jnp.float32


def loop(count, body):
    if count <= FEW:
        for i in range(count):
            body(i)
    else:
        lax.fori_loop(0, count, lambda i, _: (body(i), 0)[1], 0)


class Plan:
    def __init__(self, n_col, n_row, slots, tile, chunks):
        self.n_col, self.n_row, self.slots, self.tile = n_col, n_row, slots, tile
        self.rows = BLOCK_COLS * n_col // n_row
        self.canonical = self.rows * ROW_MOST <= slots
        self.chunks = chunks if self.canonical and self.rows % chunks == 0 else 1
        self.pos = self.rows * ROW_MOST if self.canonical else slots
        self.rc = self.rows // self.chunks
        self.pc = self.pos // self.chunks
        self.ch = self.pc * tile + META
        self.places = self.rows * BLOCK_COLS
        self.small = self.canonical and self.rows == BLOCK_COLS and n_col <= FEW
        self.width = BLOCK_COLS * tile
        assert self.pc <= META and self.places <= 256 and n_row % 2 == 0


def slot_keys(plan, idx):
    rows = [idx[0, 0, 0, s] for s in range(plan.slots)]
    out = []
    if not plan.canonical:
        for s in range(plan.slots):
            out.append((s, jnp.where(rows[s] >= 0, rows[s] * BLOCK_COLS + idx[0, 0, 1, s], -1)))
        return out
    for i in range(plan.rows):
        found = [jnp.int32(plan.slots)] * ROW_MOST
        for s in reversed(range(plan.slots)):
            hit = rows[s] == i
            found = [
                jnp.where(hit, found[k - 1] if k else jnp.int32(s), found[k]) for k in range(ROW_MOST)
            ]
        for slot in found:
            live = slot < plan.slots
            slot = jnp.minimum(slot, plan.slots - 1)
            out.append((slot, jnp.where(live, i * BLOCK_COLS + idx[0, 0, 1, slot], -1)))
    return out


def out_keys(plan, idx):
    rows = [idx[0, 0, 0, s] for s in range(plan.slots)]
    return [
        jnp.where(rows[s] >= 0, rows[s] * BLOCK_COLS + idx[0, 0, 1, s], plan.places)
        for s in range(plan.slots)
    ]


def meta_of(plan, keys):
    place = lax.broadcasted_iota(jnp.int32, (META, plan.tile), 0)
    meta = jnp.full((META, plan.tile), -1, jnp.int32)
    for p, key in enumerate(keys):
        meta = jnp.where(place == p, key, meta)
    return meta.astype(F32).astype(BF16)


def row_tiles(plan, chunk, i, il):
    t = plan.tile
    meta = chunk[plan.pc * t : plan.pc * t + META, :].astype(F32)
    cands = range(il * ROW_MOST, (il + 1) * ROW_MOST) if plan.canonical else range(plan.pc)
    out = []
    for j in range(BLOCK_COLS):
        key = jnp.asarray(i * BLOCK_COLS + j, jnp.int32).astype(F32)
        total = None
        for p in cands:
            here = jnp.broadcast_to(meta[p : p + 1, :], (META, t)) == key
            mask = jnp.where(here, 1.0, 0.0).astype(BF16)
            part = chunk[p * t : (p + 1) * t, :].reshape(t // META, META, t) * mask[None]
            total = part if total is None else total + part
        out.append(total.reshape(t, t))
    return out


def kernel(
    plan,
    x_in, xi_in, si_in, ni_in,
    sq_ref, rf_ref,
    x_ref, xi_ref, si_ref, ni_ref, local_sem,
    pk, sk, zbuf, rbuf, sbuf, bd, ld, acc, xt, *rest,
):
    if plan.small:
        sd, acc2, *sems = rest
    else:
        sd, acc2, sems = bd, acc, rest
    zrecv, up_send, dn_send, rrecv, pair_send, cross_send, relay_send, srecv, spair_send, scross_send, srelay_send = sems
    n_col, n_row, t, chunks = plan.n_col, plan.n_row, plan.tile, plan.chunks
    c = lax.axis_index("col")
    r = lax.axis_index("row")
    pair = r + 1 - 2 * lax.rem(r, 2)
    hops = range(1, n_row // 2)
    crosses = [lax.rem(r + 2 * m, n_row) for m in hops]
    sources = [lax.rem(r + n_row - 2 * m, n_row) for m in hops]
    relayed = [lax.rem(pair + n_row - 2 * m, n_row) for m in hops]

    takes = [
        pltpu.make_async_copy(src, dst, local_sem.at[n])
        for n, (src, dst) in enumerate(((xi_in, xi_ref), (x_in, x_ref), (si_in, si_ref), (ni_in, ni_ref)))
    ]
    for take in takes:
        take.start()
    barrier = pltpu.get_barrier_semaphore()

    @pl.when(c > 0)
    def _():
        pl.semaphore_signal(barrier, inc=1, device_id={"col": c - 1}, device_id_type=MESH)

    @pl.when(c < n_col - 1)
    def _():
        pl.semaphore_signal(barrier, inc=1, device_id={"col": c + 1}, device_id_type=MESH)

    for other in [pair] + crosses:
        pl.semaphore_signal(barrier, inc=1, device_id={"row": other}, device_id_type=MESH)

    takes[0].wait()
    x_keys = slot_keys(plan, xi_ref)
    takes[1].wait()
    for g in range(chunks):
        mine = x_keys[g * plan.pc : (g + 1) * plan.pc]
        for p, (slot, _) in enumerate(mine):
            pk[g, p * t : (p + 1) * t, :] = x_ref[0, 0, slot]
        pk[g, plan.pc * t : plan.ch, :] = meta_of(plan, [key for _, key in mine])

    inner = jnp.where(c > 0, 1, 0) + jnp.where(c < n_col - 1, 1, 0)
    pl.semaphore_wait(barrier, inner + 1 + len(crosses))

    def col_copy(src, kb, g, send, to):
        return pltpu.make_async_remote_copy(
            src_ref=src, dst_ref=zbuf.at[kb, g], send_sem=send.at[kb, g], recv_sem=zrecv.at[kb, g],
            device_id={"col": to}, device_id_type=MESH,
        )

    def row_copy(src, dst, origin, g, send, recv, to):
        return pltpu.make_async_remote_copy(
            src_ref=src, dst_ref=dst.at[origin, g], send_sem=send, recv_sem=recv.at[origin, g],
            device_id={"row": to}, device_id_type=MESH,
        )

    def send_row(src, dst, g, pair_sem, cross_sem, recv):
        for m, to in enumerate(crosses):
            row_copy(src.at[g], dst, r, g, cross_sem.at[m, g], recv, to).start()
        row_copy(src.at[g], dst, r, g, pair_sem.at[g], recv, pair).start()

    def take_cross(dst, g, relay_sem, recv):
        for m, origin in enumerate(sources):
            hop = row_copy(dst.at[origin, g], dst, origin, g, relay_sem.at[m, g], recv, pair)
            hop.wait_recv()
            hop.start()

    def take_pair(dst, g, recv, relay_sem):
        row_copy(dst.at[pair, g], dst, pair, g, relay_sem.at[0, g], recv, pair).wait_recv()

    def take_relayed(dst, g, recv, relay_sem):
        for origin in relayed:
            row_copy(dst.at[origin, g], dst, origin, g, relay_sem.at[0, g], recv, pair).wait_recv()

    def end_row(src, dst, g, pair_sem, cross_sem, relay_sem, recv):
        row_copy(src.at[g], dst, r, g, pair_sem.at[g], recv, pair).wait_send()
        for m, to in enumerate(crosses):
            row_copy(src.at[g], dst, r, g, cross_sem.at[m, g], recv, to).wait_send()
        for m, origin in enumerate(sources):
            row_copy(dst.at[origin, g], dst, origin, g, relay_sem.at[m, g], recv, pair).wait_send()

    for g in range(chunks):
        @pl.when(c < n_col - 1)
        def _():
            col_copy(pk.at[g], c, g, up_send, c + 1).start()

        @pl.when(c > 0)
        def _():
            col_copy(pk.at[g], c, g, dn_send, c - 1).start()

        send_row(pk, rbuf, g, pair_send, cross_send, rrecv)

    acc[plan.places] = jnp.zeros((t, t), F32)
    acc2[plan.places] = jnp.zeros((t, t), F32)
    xt[plan.places] = jnp.zeros((t, t), BF16)

    def forward(d, g):
        @pl.when(c >= d)
        def _():
            col_copy(zbuf.at[c - d, g], c - d, g, up_send, c).wait_recv()

            @pl.when(c < n_col - 1)
            def _():
                col_copy(zbuf.at[c - d, g], c - d, g, up_send, c + 1).start()

        @pl.when(c + d < n_col)
        def _():
            col_copy(zbuf.at[c + d, g], c + d, g, dn_send, c).wait_recv()

            @pl.when(c > 0)
            def _():
                col_copy(zbuf.at[c + d, g], c + d, g, dn_send, c - 1).start()

    def unpack(chunk, origin, g, dense):
        def one(il):
            i = g * plan.rc + il
            for j, tile in enumerate(row_tiles(plan, chunk, i, il)):
                dense[origin * plan.rows + i, :, j * t : (j + 1) * t] = tile
        loop(plan.rc, one)

    def right_of(dense, kb):
        return dense[pl.ds(kb * BLOCK_COLS, BLOCK_COLS)].reshape(plan.width, plan.width)

    def add(into, i, product, first):
        for j in range(BLOCK_COLS):
            part = product[:, j * t : (j + 1) * t]
            if first:
                into[i * BLOCK_COLS + j] = part
            else:
                into[i * BLOCK_COLS + j] += part

    def multiply(chunk, kb, g, dense, into, first):
        def one(il):
            i = g * plan.rc + il
            left = jnp.concatenate(row_tiles(plan, chunk, i, il), axis=1)
            add(into, i, jnp.dot(left, right_of(dense, kb), preferred_element_type=F32), first)

        if not plan.small:
            loop(plan.rc, one)
            return
        for il in range(plan.rc):
            for j, tile in enumerate(row_tiles(plan, chunk, g * plan.rc + il, il)):
                part, at = divmod(j, plan.rc)
                ld[part, kb, g * plan.rc + il, :, at * t : (at + 1) * t] = tile
        left = jnp.concatenate(
            [
                ld[part, kb, g * plan.rc : (g + 1) * plan.rc].reshape(plan.rc * t, plan.rc * t)
                for part in range(chunks)
            ],
            axis=1,
        )
        product = jnp.dot(left, right_of(dense, kb), preferred_element_type=F32)
        for il in range(plan.rc):
            add(into, g * plan.rc + il, product[il * t : (il + 1) * t], first)

    def multiply_pair(d, g, dense, into):
        @pl.when(c >= d)
        def _():
            multiply(zbuf.at[c - d, g], c - d, g, dense, into, False)

        @pl.when(c + d < n_col)
        def _():
            multiply(zbuf.at[c + d, g], c + d, g, dense, into, False)

    for g in range(chunks):
        take_cross(rbuf, g, relay_send, rrecv)
        forward(1, g)
    for g in range(chunks):
        unpack(pk.at[g], r, g, bd)
        take_pair(rbuf, g, rrecv, relay_send)
        unpack(rbuf.at[pair, g], pair, g, bd)
        for origin in sources:
            unpack(rbuf.at[origin, g], origin, g, bd)

        def keep(il):
            i = g * plan.rc + il
            for j in range(BLOCK_COLS):
                xt[i * BLOCK_COLS + j] = bd[r * plan.rows + i, :, j * t : (j + 1) * t]
        loop(plan.rc, keep)
    for g in range(chunks):
        take_relayed(rbuf, g, rrecv, relay_send)
        for origin in relayed:
            unpack(rbuf.at[origin, g], origin, g, bd)
    for g in range(chunks):
        multiply(pk.at[g], c, g, bd, acc, True)

    takes[2].wait()
    takes[3].wait()
    s_keys = slot_keys(plan, si_ref)

    def send_square(g):
        mine = s_keys[g * plan.pc : (g + 1) * plan.pc]
        for p, (_, key) in enumerate(mine):
            sk[g, p * t : (p + 1) * t, :] = acc[jnp.where(key < 0, plan.places, key)].astype(BF16)
        sk[g, plan.pc * t : plan.ch, :] = meta_of(plan, [key for _, key in mine])
        send_row(sk, sbuf, g, spair_send, scross_send, srecv)

    for g in range(chunks):
        multiply_pair(1, g, bd, acc)

    if plan.small:
        for d in range(2, n_col):
            for g in range(chunks):
                forward(d, g)
                multiply_pair(d, g, bd, acc)
                if d == n_col - 1:
                    send_square(g)
        if n_col == 2:
            for g in range(chunks):
                send_square(g)
    else:
        def later(d):
            for g in range(chunks):
                forward(d, g)
                multiply_pair(d, g, bd, acc)
        lax.fori_loop(2, n_col, lambda d, _: (later(d), 0)[1], 0)
        for g in range(chunks):
            send_square(g)

    for s, key in enumerate(out_keys(plan, si_ref)):
        sq_ref[0, 0, s] = acc[key].astype(BF16)

    def add_square(g):
        left = jnp.concatenate(
            [ld[g, kb].reshape(plan.rows * t, plan.rc * t) for kb in range(n_col)], axis=1
        )
        right = jnp.concatenate(
            [
                sd[kb * plan.rows + g * plan.rc : kb * plan.rows + (g + 1) * plan.rc].reshape(
                    plan.rc * t, plan.width
                )
                for kb in range(n_col)
            ],
            axis=0,
        )
        product = jnp.dot(left, right, preferred_element_type=F32)
        for i in range(plan.rows):
            add(acc2, i, product[i * t : (i + 1) * t], g == 0)

    def take_square(g):
        unpack(sk.at[g], r, g, sd)
        take_pair(sbuf, g, srecv, srelay_send)
        unpack(sbuf.at[pair, g], pair, g, sd)
        for origin in sources:
            unpack(sbuf.at[origin, g], origin, g, sd)
        take_relayed(sbuf, g, srecv, srelay_send)
        for origin in relayed:
            unpack(sbuf.at[origin, g], origin, g, sd)

    for g in range(chunks - 1):
        take_cross(sbuf, g, srelay_send, srecv)
    for g in range(chunks - 1):
        take_square(g)
        if plan.small:
            add_square(g)
    take_cross(sbuf, chunks - 1, srelay_send, srecv)
    take_square(chunks - 1)
    if plan.small:
        add_square(chunks - 1)
    else:
        for g in range(chunks):
            multiply(pk.at[g], c, g, sd, acc2, True)

            def again(d):
                multiply_pair(d, g, sd, acc2)
            lax.fori_loop(1, n_col, lambda d, _: (again(d), 0)[1], 0)

    for s, key in enumerate(out_keys(plan, ni_ref)):
        rf_ref[0, 0, s] = (1.5 * xt[key].astype(F32) - 0.5 * acc2[key]).astype(BF16)

    for g in range(chunks):
        end_row(pk, rbuf, g, pair_send, cross_send, relay_send, rrecv)
        end_row(sk, sbuf, g, spair_send, scross_send, srelay_send, srecv)

        @pl.when(c < n_col - 1)
        def _():
            col_copy(pk.at[g], c, g, up_send, c + 1).wait_send()

        @pl.when(c > 0)
        def _():
            col_copy(pk.at[g], c, g, dn_send, c - 1).wait_send()

        def sent(d):
            @pl.when(jnp.logical_and(c >= d, c < n_col - 1))
            def _():
                col_copy(zbuf.at[c - d, g], c - d, g, up_send, c + 1).wait_send()

            @pl.when(jnp.logical_and(c + d < n_col, c > 0))
            def _():
                col_copy(zbuf.at[c + d, g], c + d, g, dn_send, c - 1).wait_send()
        if plan.small:
            for d in range(1, n_col):
                sent(d)
        else:
            lax.fori_loop(1, n_col, lambda d, _: (sent(d), 0)[1], 0)


CHUNKS = 4


def solution(mesh):
    n_col, n_row = mesh.shape["col"], mesh.shape["row"]

    def shards(x_tiles, x_index, square_index, new_index):
        slots, t = x_tiles.shape[2], x_tiles.shape[3]
        plan = Plan(n_col, n_row, slots, t, CHUNKS)
        k, ch, g = plan.rows * n_row, plan.ch, plan.chunks
        half = max(n_row // 2 - 1, 1)
        scratch = [
            pltpu.VMEM(x_tiles.shape, BF16),
            pltpu.SMEM(x_index.shape, jnp.int32),
            pltpu.SMEM(x_index.shape, jnp.int32),
            pltpu.SMEM(x_index.shape, jnp.int32),
            pltpu.SemaphoreType.DMA((6,)),
            pltpu.VMEM((g, ch, t), BF16),
            pltpu.VMEM((g, ch, t), BF16),
            pltpu.VMEM((n_col, g, ch, t), BF16),
            pltpu.VMEM((n_row, g, ch, t), BF16),
            pltpu.VMEM((n_row, g, ch, t), BF16),
            pltpu.VMEM((k, t, plan.width), BF16),
            pltpu.VMEM((g, n_col, plan.rows, t, plan.rc * t) if plan.small else (1, 1, 1, 16, t), BF16),
            pltpu.VMEM((plan.places + 1, t, t), F32),
            pltpu.VMEM((plan.places + 1, t, t), BF16),
        ]
        if plan.small:
            scratch += [
                pltpu.VMEM((k, t, plan.width), BF16),
                pltpu.VMEM((plan.places + 1, t, t), F32),
            ]
        dma = pltpu.SemaphoreType.DMA
        scratch += [dma((n_col, g))] * 3
        scratch += [dma((n_row, g)), dma((g,)), dma((half, g)), dma((half, g))] * 2
        shape = jax.ShapeDtypeStruct(x_tiles.shape, BF16)
        whole = pl.BlockSpec(memory_space=pltpu.HBM)
        there = pl.BlockSpec(memory_space=pltpu.VMEM)
        return pl.pallas_call(
            functools.partial(kernel, plan),
            out_shape=(shape, shape),
            in_specs=[whole] * 4,
            out_specs=(there, there),
            scratch_shapes=scratch,
            compiler_params=pltpu.CompilerParams(
                collective_id=0, has_side_effects=True,
                vmem_limit_bytes=(62 if plan.small else 56) * 2**20,
            ),
        )(x_tiles, x_index, square_index, new_index)

    tiles = P(("parts", "row"), "col", None, None, None)
    index = P(("parts", "row"), "col", None, None)
    return jax.shard_map(
        shards, mesh=mesh, in_specs=(tiles, index, index, index), out_specs=(tiles, tiles), check_vma=False,
    )
```

```python
import functools

import jax
import jax.numpy as jnp
from jax import lax
from jax.experimental import pallas as pl
from jax.experimental.pallas import tpu as pltpu
from jax.sharding import PartitionSpec as P

MESH = pl.DeviceIdType.MESH
ROW_MOST = 2
BLOCK_COLS = 4
META = 16
FEW = 8
BF16 = jnp.bfloat16
F32 = jnp.float32


def loop(count, body):
    if count <= FEW:
        for i in range(count):
            body(i)
    else:
        lax.fori_loop(0, count, lambda i, _: (body(i), 0)[1], 0)


class Plan:
    def __init__(self, n_col, n_row, slots, tile, chunks):
        self.n_col, self.n_row, self.slots, self.tile = n_col, n_row, slots, tile
        self.rows = BLOCK_COLS * n_col // n_row
        self.canonical = self.rows * ROW_MOST <= slots
        self.chunks = chunks if self.canonical and self.rows % chunks == 0 else 1
        self.pos = self.rows * ROW_MOST if self.canonical else slots
        self.rc = self.rows // self.chunks
        self.pc = self.pos // self.chunks
        self.ch = self.pc * tile + META
        self.places = self.rows * BLOCK_COLS
        self.small = self.canonical and self.rows == BLOCK_COLS and n_col <= FEW
        self.width = BLOCK_COLS * tile
        assert self.pc <= META and self.places <= 256 and n_row % 2 == 0


def slot_keys(plan, idx):
    rows = [idx[0, 0, 0, s] for s in range(plan.slots)]
    out = []
    if not plan.canonical:
        for s in range(plan.slots):
            out.append((s, jnp.where(rows[s] >= 0, rows[s] * BLOCK_COLS + idx[0, 0, 1, s], -1)))
        return out
    for i in range(plan.rows):
        found = [jnp.int32(plan.slots)] * ROW_MOST
        for s in reversed(range(plan.slots)):
            hit = rows[s] == i
            found = [
                jnp.where(hit, found[k - 1] if k else jnp.int32(s), found[k]) for k in range(ROW_MOST)
            ]
        for slot in found:
            live = slot < plan.slots
            slot = jnp.minimum(slot, plan.slots - 1)
            out.append((slot, jnp.where(live, i * BLOCK_COLS + idx[0, 0, 1, slot], -1)))
    return out


def out_keys(plan, idx):
    rows = [idx[0, 0, 0, s] for s in range(plan.slots)]
    return [
        jnp.where(rows[s] >= 0, rows[s] * BLOCK_COLS + idx[0, 0, 1, s], plan.places)
        for s in range(plan.slots)
    ]


def meta_of(plan, keys):
    place = lax.broadcasted_iota(jnp.int32, (META, plan.tile), 0)
    meta = jnp.full((META, plan.tile), -1, jnp.int32)
    for p, key in enumerate(keys):
        meta = jnp.where(place == p, key, meta)
    return meta.astype(F32).astype(BF16)


def row_tiles(plan, chunk, i, il):
    t = plan.tile
    meta = chunk[plan.pc * t : plan.pc * t + META, :].astype(F32)
    cands = range(il * ROW_MOST, (il + 1) * ROW_MOST) if plan.canonical else range(plan.pc)
    out = []
    for j in range(BLOCK_COLS):
        key = jnp.asarray(i * BLOCK_COLS + j, jnp.int32).astype(F32)
        total = None
        for p in cands:
            here = jnp.broadcast_to(meta[p : p + 1, :], (META, t)) == key
            mask = jnp.where(here, 1.0, 0.0).astype(BF16)
            part = chunk[p * t : (p + 1) * t, :].reshape(t // META, META, t) * mask[None]
            total = part if total is None else total + part
        out.append(total.reshape(t, t))
    return out


def kernel(
    plan,
    x_in, xi_in, si_in, ni_in,
    sq_ref, rf_ref,
    x_ref, xi_ref, si_ref, ni_ref, local_sem,
    pk, sk, zbuf, rbuf, sbuf, bd, ld, acc, xt, *rest,
):
    if plan.small:
        sd, acc2, *sems = rest
    else:
        sd, acc2, sems = bd, acc, rest
    zrecv, up_send, dn_send, rrecv, pair_send, cross_send, relay_send, srecv, spair_send, scross_send, srelay_send = sems
    n_col, n_row, t, chunks = plan.n_col, plan.n_row, plan.tile, plan.chunks
    c = lax.axis_index("col")
    r = lax.axis_index("row")
    pair = r + 1 - 2 * lax.rem(r, 2)
    hops = range(1, n_row // 2)
    crosses = [lax.rem(r + 2 * m, n_row) for m in hops]
    sources = [lax.rem(r + n_row - 2 * m, n_row) for m in hops]
    relayed = [lax.rem(pair + n_row - 2 * m, n_row) for m in hops]

    takes = [
        pltpu.make_async_copy(src, dst, local_sem.at[n])
        for n, (src, dst) in enumerate(((xi_in, xi_ref), (x_in, x_ref), (si_in, si_ref), (ni_in, ni_ref)))
    ]
    for take in takes:
        take.start()
    barrier = pltpu.get_barrier_semaphore()

    @pl.when(c > 0)
    def _():
        pl.semaphore_signal(barrier, inc=1, device_id={"col": c - 1}, device_id_type=MESH)

    @pl.when(c < n_col - 1)
    def _():
        pl.semaphore_signal(barrier, inc=1, device_id={"col": c + 1}, device_id_type=MESH)

    for other in [pair] + crosses:
        pl.semaphore_signal(barrier, inc=1, device_id={"row": other}, device_id_type=MESH)

    takes[0].wait()
    x_keys = slot_keys(plan, xi_ref)
    takes[1].wait()
    for g in range(chunks):
        mine = x_keys[g * plan.pc : (g + 1) * plan.pc]
        for p, (slot, _) in enumerate(mine):
            pk[g, p * t : (p + 1) * t, :] = x_ref[0, 0, slot]
        pk[g, plan.pc * t : plan.ch, :] = meta_of(plan, [key for _, key in mine])

    inner = jnp.where(c > 0, 1, 0) + jnp.where(c < n_col - 1, 1, 0)
    pl.semaphore_wait(barrier, inner + 1 + len(crosses))

    def col_copy(src, kb, g, send, to):
        return pltpu.make_async_remote_copy(
            src_ref=src, dst_ref=zbuf.at[kb, g], send_sem=send.at[kb, g], recv_sem=zrecv.at[kb, g],
            device_id={"col": to}, device_id_type=MESH,
        )

    def row_copy(src, dst, origin, g, send, recv, to):
        return pltpu.make_async_remote_copy(
            src_ref=src, dst_ref=dst.at[origin, g], send_sem=send, recv_sem=recv.at[origin, g],
            device_id={"row": to}, device_id_type=MESH,
        )

    def send_row(src, dst, g, pair_sem, cross_sem, recv):
        for m, to in enumerate(crosses):
            row_copy(src.at[g], dst, r, g, cross_sem.at[m, g], recv, to).start()
        row_copy(src.at[g], dst, r, g, pair_sem.at[g], recv, pair).start()

    def take_cross(dst, g, relay_sem, recv):
        for m, origin in enumerate(sources):
            hop = row_copy(dst.at[origin, g], dst, origin, g, relay_sem.at[m, g], recv, pair)
            hop.wait_recv()
            hop.start()

    def take_pair(dst, g, recv, relay_sem):
        row_copy(dst.at[pair, g], dst, pair, g, relay_sem.at[0, g], recv, pair).wait_recv()

    def take_relayed(dst, g, recv, relay_sem):
        for origin in relayed:
            row_copy(dst.at[origin, g], dst, origin, g, relay_sem.at[0, g], recv, pair).wait_recv()

    def end_row(src, dst, g, pair_sem, cross_sem, relay_sem, recv):
        row_copy(src.at[g], dst, r, g, pair_sem.at[g], recv, pair).wait_send()
        for m, to in enumerate(crosses):
            row_copy(src.at[g], dst, r, g, cross_sem.at[m, g], recv, to).wait_send()
        for m, origin in enumerate(sources):
            row_copy(dst.at[origin, g], dst, origin, g, relay_sem.at[m, g], recv, pair).wait_send()

    for g in range(chunks):
        @pl.when(c < n_col - 1)
        def _():
            col_copy(pk.at[g], c, g, up_send, c + 1).start()

        @pl.when(c > 0)
        def _():
            col_copy(pk.at[g], c, g, dn_send, c - 1).start()

    for g in range(chunks):
        send_row(pk, rbuf, g, pair_send, cross_send, rrecv)

    acc[plan.places] = jnp.zeros((t, t), F32)
    acc2[plan.places] = jnp.zeros((t, t), F32)
    xt[plan.places] = jnp.zeros((t, t), BF16)

    def forward(d, g):
        @pl.when(c >= d)
        def _():
            col_copy(zbuf.at[c - d, g], c - d, g, up_send, c).wait_recv()

            @pl.when(c < n_col - 1)
            def _():
                col_copy(zbuf.at[c - d, g], c - d, g, up_send, c + 1).start()

        @pl.when(c + d < n_col)
        def _():
            col_copy(zbuf.at[c + d, g], c + d, g, dn_send, c).wait_recv()

            @pl.when(c > 0)
            def _():
                col_copy(zbuf.at[c + d, g], c + d, g, dn_send, c - 1).start()

    def unpack(chunk, origin, g, dense):
        def one(il):
            i = g * plan.rc + il
            for j, tile in enumerate(row_tiles(plan, chunk, i, il)):
                dense[origin * plan.rows + i, :, j * t : (j + 1) * t] = tile
        loop(plan.rc, one)

    def right_of(dense, kb):
        return dense[pl.ds(kb * BLOCK_COLS, BLOCK_COLS)].reshape(plan.width, plan.width)

    def add(into, i, product, first):
        for j in range(BLOCK_COLS):
            part = product[:, j * t : (j + 1) * t]
            if first:
                into[i * BLOCK_COLS + j] = part
            else:
                into[i * BLOCK_COLS + j] += part

    def multiply(chunk, kb, g, dense, into, first):
        def one(il):
            i = g * plan.rc + il
            left = jnp.concatenate(row_tiles(plan, chunk, i, il), axis=1)
            add(into, i, jnp.dot(left, right_of(dense, kb), preferred_element_type=F32), first)

        if not plan.small:
            loop(plan.rc, one)
            return
        for il in range(plan.rc):
            for j, tile in enumerate(row_tiles(plan, chunk, g * plan.rc + il, il)):
                part, at = divmod(j, plan.rc)
                ld[part, kb, g * plan.rc + il, :, at * t : (at + 1) * t] = tile
        left = jnp.concatenate(
            [
                ld[part, kb, g * plan.rc : (g + 1) * plan.rc].reshape(plan.rc * t, plan.rc * t)
                for part in range(chunks)
            ],
            axis=1,
        )
        product = jnp.dot(left, right_of(dense, kb), preferred_element_type=F32)
        for il in range(plan.rc):
            add(into, g * plan.rc + il, product[il * t : (il + 1) * t], first)

    def multiply_pair(d, g, dense, into):
        @pl.when(c >= d)
        def _():
            multiply(zbuf.at[c - d, g], c - d, g, dense, into, False)

        @pl.when(c + d < n_col)
        def _():
            multiply(zbuf.at[c + d, g], c + d, g, dense, into, False)

    for g in range(chunks):
        take_cross(rbuf, g, relay_send, rrecv)
        forward(1, g)
    for g in range(chunks):
        unpack(pk.at[g], r, g, bd)
        take_pair(rbuf, g, rrecv, relay_send)
        unpack(rbuf.at[pair, g], pair, g, bd)
        for origin in sources:
            unpack(rbuf.at[origin, g], origin, g, bd)

        def keep(il):
            i = g * plan.rc + il
            for j in range(BLOCK_COLS):
                xt[i * BLOCK_COLS + j] = bd[r * plan.rows + i, :, j * t : (j + 1) * t]
        loop(plan.rc, keep)
    for g in range(chunks):
        take_relayed(rbuf, g, rrecv, relay_send)
        for origin in relayed:
            unpack(rbuf.at[origin, g], origin, g, bd)
    for g in range(chunks):
        multiply(pk.at[g], c, g, bd, acc, True)

    takes[2].wait()
    takes[3].wait()
    s_keys = slot_keys(plan, si_ref)

    def send_square(g):
        mine = s_keys[g * plan.pc : (g + 1) * plan.pc]
        for p, (_, key) in enumerate(mine):
            sk[g, p * t : (p + 1) * t, :] = acc[jnp.where(key < 0, plan.places, key)].astype(BF16)
        sk[g, plan.pc * t : plan.ch, :] = meta_of(plan, [key for _, key in mine])
        send_row(sk, sbuf, g, spair_send, scross_send, srecv)

    for g in range(chunks):
        multiply_pair(1, g, bd, acc)

    if plan.small:
        for d in range(2, n_col):
            for g in range(chunks):
                forward(d, g)
                multiply_pair(d, g, bd, acc)
                if d == n_col - 1:
                    send_square(g)
        if n_col == 2:
            for g in range(chunks):
                send_square(g)
    else:
        def later(d):
            for g in range(chunks):
                forward(d, g)
                multiply_pair(d, g, bd, acc)
        lax.fori_loop(2, n_col, lambda d, _: (later(d), 0)[1], 0)
        for g in range(chunks):
            send_square(g)

    for s, key in enumerate(out_keys(plan, si_ref)):
        sq_ref[0, 0, s] = acc[key].astype(BF16)

    def add_square(g):
        left = jnp.concatenate(
            [ld[g, kb].reshape(plan.rows * t, plan.rc * t) for kb in range(n_col)], axis=1
        )
        right = jnp.concatenate(
            [
                sd[kb * plan.rows + g * plan.rc : kb * plan.rows + (g + 1) * plan.rc].reshape(
                    plan.rc * t, plan.width
                )
                for kb in range(n_col)
            ],
            axis=0,
        )
        product = jnp.dot(left, right, preferred_element_type=F32)
        for i in range(plan.rows):
            add(acc2, i, product[i * t : (i + 1) * t], g == 0)

    def take_square(g):
        unpack(sk.at[g], r, g, sd)
        take_pair(sbuf, g, srecv, srelay_send)
        unpack(sbuf.at[pair, g], pair, g, sd)
        for origin in sources:
            unpack(sbuf.at[origin, g], origin, g, sd)
        take_relayed(sbuf, g, srecv, srelay_send)
        for origin in relayed:
            unpack(sbuf.at[origin, g], origin, g, sd)

    for g in range(chunks - 1):
        take_cross(sbuf, g, srelay_send, srecv)
    for g in range(chunks - 1):
        take_square(g)
        if plan.small:
            add_square(g)
    take_cross(sbuf, chunks - 1, srelay_send, srecv)
    take_square(chunks - 1)
    if plan.small:
        add_square(chunks - 1)
    else:
        for g in range(chunks):
            multiply(pk.at[g], c, g, sd, acc2, True)

            def again(d):
                multiply_pair(d, g, sd, acc2)
            lax.fori_loop(1, n_col, lambda d, _: (again(d), 0)[1], 0)

    for s, key in enumerate(out_keys(plan, ni_ref)):
        rf_ref[0, 0, s] = (1.5 * xt[key].astype(F32) - 0.5 * acc2[key]).astype(BF16)

    for g in range(chunks):
        end_row(pk, rbuf, g, pair_send, cross_send, relay_send, rrecv)
        end_row(sk, sbuf, g, spair_send, scross_send, srelay_send, srecv)

        @pl.when(c < n_col - 1)
        def _():
            col_copy(pk.at[g], c, g, up_send, c + 1).wait_send()

        @pl.when(c > 0)
        def _():
            col_copy(pk.at[g], c, g, dn_send, c - 1).wait_send()

        def sent(d):
            @pl.when(jnp.logical_and(c >= d, c < n_col - 1))
            def _():
                col_copy(zbuf.at[c - d, g], c - d, g, up_send, c + 1).wait_send()

            @pl.when(jnp.logical_and(c + d < n_col, c > 0))
            def _():
                col_copy(zbuf.at[c + d, g], c + d, g, dn_send, c - 1).wait_send()
        if plan.small:
            for d in range(1, n_col):
                sent(d)
        else:
            lax.fori_loop(1, n_col, lambda d, _: (sent(d), 0)[1], 0)


CHUNKS = 4


def solution(mesh):
    n_col, n_row = mesh.shape["col"], mesh.shape["row"]

    def shards(x_tiles, x_index, square_index, new_index):
        slots, t = x_tiles.shape[2], x_tiles.shape[3]
        plan = Plan(n_col, n_row, slots, t, CHUNKS)
        k, ch, g = plan.rows * n_row, plan.ch, plan.chunks
        half = max(n_row // 2 - 1, 1)
        scratch = [
            pltpu.VMEM(x_tiles.shape, BF16),
            pltpu.SMEM(x_index.shape, jnp.int32),
            pltpu.SMEM(x_index.shape, jnp.int32),
            pltpu.SMEM(x_index.shape, jnp.int32),
            pltpu.SemaphoreType.DMA((6,)),
            pltpu.VMEM((g, ch, t), BF16),
            pltpu.VMEM((g, ch, t), BF16),
            pltpu.VMEM((n_col, g, ch, t), BF16),
            pltpu.VMEM((n_row, g, ch, t), BF16),
            pltpu.VMEM((n_row, g, ch, t), BF16),
            pltpu.VMEM((k, t, plan.width), BF16),
            pltpu.VMEM((g, n_col, plan.rows, t, plan.rc * t) if plan.small else (1, 1, 1, 16, t), BF16),
            pltpu.VMEM((plan.places + 1, t, t), F32),
            pltpu.VMEM((plan.places + 1, t, t), BF16),
        ]
        if plan.small:
            scratch += [
                pltpu.VMEM((k, t, plan.width), BF16),
                pltpu.VMEM((plan.places + 1, t, t), F32),
            ]
        dma = pltpu.SemaphoreType.DMA
        scratch += [dma((n_col, g))] * 3
        scratch += [dma((n_row, g)), dma((g,)), dma((half, g)), dma((half, g))] * 2
        shape = jax.ShapeDtypeStruct(x_tiles.shape, BF16)
        whole = pl.BlockSpec(memory_space=pltpu.HBM)
        there = pl.BlockSpec(memory_space=pltpu.VMEM)
        return pl.pallas_call(
            functools.partial(kernel, plan),
            out_shape=(shape, shape),
            in_specs=[whole] * 4,
            out_specs=(there, there),
            scratch_shapes=scratch,
            compiler_params=pltpu.CompilerParams(
                collective_id=0, has_side_effects=True,
                vmem_limit_bytes=(62 if plan.small else 56) * 2**20,
            ),
        )(x_tiles, x_index, square_index, new_index)

    tiles = P(("parts", "row"), "col", None, None, None)
    index = P(("parts", "row"), "col", None, None)
    return jax.shard_map(
        shards, mesh=mesh, in_specs=(tiles, index, index, index), out_specs=(tiles, tiles), check_vma=False,
    )
```
